256 devices in a mesh: rep: 8 (over y, core), grp: 32 (over z, x).
Axes of the slice: x: 4, y: 4, z: 8, core: 2. Of those that a mesh axis runs over, the one named last changes fastest.
Arguments:
- amps: float32 [8, 1024, 32768], P(None, None, ('rep', 'grp')), may hold values from -0.125 to 0.125
- integrals: float32 [8, 32768, 512], P(None, 'rep', 'grp'), may hold values from -6 to 6
- residual_other: float32 [1024, 8, 512], P(('rep', 'grp')), may hold values from -6 to 6
- row_gap: float32 [1024, 8], P(('rep', 'grp')), may hold values from 0.5 to 4
- col_gap: float32 [8, 512], replicated, may hold values from 0.5 to 4
- row_count: int32 [8], replicated, may hold values from 1 to 1024, 6144 in all
- k_count: int32 [8], replicated, may hold values from 1 to 32768, 196608 in all
- col_count: int32 [8], replicated, may hold values from 1 to 512, 3072 in all
Outputs:
- update: float32 [1024, 8, 512], P(('rep', 'grp'))
The draws below stay inside these ranges and needn't reach their ends.
Inputs may be any that keep to these rules, and one draw needn't show every extreme that they name: `row_count`: live rows of the irreps sum to 6144; one irrep has exactly 1024. `k_count`: live summed pairs of the irreps sum to 196608; one irrep has exactly 32768. `col_count`: live columns of the irreps sum to 3072; one irrep has exactly 512.
All inputs are finite; a program needn't handle non-finite values.
Results may differ from the reference program's by a relative error of at most 0.0003.
Values sent between devices are 32-bit elements; how exact they have to be, the bound alone decides.
A program may use at most 128 MiB of HBM per device.

```python
import math
import jax
import jax.numpy as jnp
import numpy as np
from jax import lax

NIRR = 8
K = 32768
M = 1024
N = 512


def spiked(drawn, key, source, target, parts, factor):
    owner, partner = [(jnp.arange(drawn.shape[axis_at]) // (drawn.shape[axis_at] // parts)).reshape([-1 if axis == axis_at else 1 for axis in range(drawn.ndim)]) for axis_at in (source, target)]
    chosen = jax.random.permutation(key, parts)[partner]
    strong = (owner == chosen) | (owner == (partner + parts // 2) % parts)
    return jnp.where(strong, factor * drawn, drawn)


def steps_of(own_key, shape, pieces, low, high):
    factor_of = 1.0
    for axis_at, shards_of in pieces:
        draws = jax.random.uniform(jax.random.fold_in(jax.random.fold_in(own_key, 6), axis_at), (shards_of,), jnp.float32, low / len(pieces), high / len(pieces))
        factor_of = factor_of * jnp.repeat(jnp.exp(draws), shape[axis_at] // shards_of).reshape((-1,) + (1,) * (len(shape) - 1 - axis_at))
    return factor_of


def profile(number_of, total, reach, lean):
    loads = [(1 << 20) // math.isqrt(standing ** lean) + 1 for standing in range(2, number_of + 1)]
    spare, counts = total - reach - (number_of - 1), [1] * (number_of - 1)
    while spare > 0:
        movable = [i for i in range(number_of - 1) if counts[i] < reach]
        pool, remaining = sum([loads[i] for i in movable]), spare
        for i in movable:
            addition = min(reach - counts[i], max(1, remaining * loads[i] // pool), spare)
            counts[i] = counts[i] + addition
            spare = spare - addition
    return np.array([reach] + counts)


def ragged(key, number_of, total, most, skew):
    if number_of == 2:
        one = jax.random.randint(key, (), max(1, total - most), min(most, total - 1) + 1)
        return jnp.stack([one, total - one])
    tallies = jnp.asarray(profile(number_of, total, most, skew), jnp.int32)
    pairs = (number_of - 1) // 2
    source_of, receiver = tallies[1:1 + 2 * pairs:2], tallies[2:2 + 2 * pairs:2]
    margin = jnp.minimum(source_of - 1, most - receiver)
    passed = jax.random.randint(jax.random.fold_in(key, 1), (pairs,), 0, 1 << 20) % (margin + 1)
    tallies = tallies.at[1:1 + 2 * pairs:2].set(source_of - passed).at[2:2 + 2 * pairs:2].set(receiver + passed)
    return tallies[jax.random.permutation(jax.random.fold_in(key, 2), number_of)]


def bell_draw(key, extent, spread, limit, cuts=(), kind=jnp.bfloat16):
    entries = spread * jax.random.normal(key, extent, jnp.float32)
    if cuts:
        entries = entries * steps_of(key, extent, cuts, -0.22, 0.18)
    return jnp.clip(entries, -limit, limit).astype(kind)


def noise_with(key, extent, deviation, most, shards, heavy, held_as=jnp.bfloat16):
    array = deviation * jax.random.normal(key, extent, jnp.float32)
    if shards:
        array = array * steps_of(key, extent, shards, -0.22, 0.18)
    return jnp.clip(spiked(array, jax.random.fold_in(key, 3), *heavy), -most, most).astype(held_as)


def setup_inputs(seed: int = 0) -> dict:
    arg_keys = jax.random.split(jax.random.key(seed), 9)
    return {
        "amps": noise_with(arg_keys[0], (NIRR, M, K), K ** -0.5, 0.125, ((2, 256),), (2, 1, 256, 6.0), jnp.float32),
        "integrals": bell_draw(arg_keys[1], (NIRR, K, N), 1.0, 6.0, ((1, 8), (2, 32)), jnp.float32),
        "residual_other": bell_draw(arg_keys[2], (M, NIRR, N), 1.0, 6.0, ((0, 256),), jnp.float32),
        "row_gap": jnp.clip(jnp.exp(math.log(4.0) - 2.0794415 * jax.random.uniform(arg_keys[3], (M, NIRR), jnp.float32) ** steps_of(arg_keys[3], (M, NIRR), ((0, 256),), -0.2, 0.2)), 0.5, 4.0),
        "col_gap": jnp.clip(jnp.exp(jax.random.uniform(arg_keys[4], (NIRR, N), jnp.float32, math.log(0.5), math.log(4.0))), 0.5, 4.0),
        "row_count": ragged(arg_keys[5], NIRR, 6 * M, M, 1).astype(jnp.int32),
        "k_count": ragged(arg_keys[6], NIRR, 6 * K, K, 1).astype(jnp.int32),
        "col_count": ragged(arg_keys[7], NIRR, 6 * N, N, 1).astype(jnp.int32),
    }


def reference(amps, integrals, residual_other, row_gap, col_gap, row_count, k_count, col_count):
    k_index = jnp.arange(K, dtype=jnp.int32)

    def one_irrep(operands):
        left_block, right_block, live_pairs = operands
        right_block = jnp.where(k_index[:, None] < live_pairs, right_block, 0.0)
        return jnp.dot(left_block, right_block, precision=lax.Precision.HIGHEST, preferred_element_type=jnp.float32)

    cycle_sum = lax.map(one_irrep, (amps, integrals, k_count))
    cycle_sum = jnp.transpose(cycle_sum, (1, 0, 2))
    row_index = jnp.arange(M, dtype=jnp.int32)[:, None, None]
    col_index = jnp.arange(N, dtype=jnp.int32)[None, None, :]
    live_mask = (row_index < row_count[None, :, None]) & (col_index < col_count[None, :, None])
    denominator = row_gap[:, :, None] + col_gap[None, :, :]
    return jnp.where(live_mask, -(cycle_sum + residual_other) / denominator, 0.0)
```

```python
import functools

import jax
import jax.numpy as jnp
from jax import lax
from jax.experimental import pallas as pl
from jax.experimental.pallas import tpu as pltpu
from jax.sharding import PartitionSpec as P

MESH = pl.DeviceIdType.MESH
NY, NC, NZ, NX = 4, 2, 8, 4
GRP = NZ * NX
NIRR = 8
ROWS = 1024
COLS = 512
KB = 128
CB = COLS // GRP
R = 4
HALF = ROWS // NC
PC = 384
QC = COLS - PC
AHEAD = 3


def kernel(
    amps, ints, k_count, out,
    blocks, lhs, rhs, c_send, c_recv,
    py_d, py_1, py_2, px_d, px_1, px_2,
    qx_d, qx_1, qx_2, qy_d, qy_1, qy_2,
    f_even, z_send, z_recv,
    x_ssem, x_rsem, c_ssem, c_rsem, p_ssem, p_rsem, z_ssem, z_rsem,
):
    rep, grp = lax.axis_index("rep"), lax.axis_index("grp")
    y, c = rep // NC, rep % NC
    z, x = grp // NX, grp % NX
    first_k = (rep * GRP + grp) * KB

    def peer(d):
        return lax.rem(z + d // NX, NZ) * NX + lax.rem(x + lax.rem(d, NX), NX)

    sibling = (y * NC + 1 - c, grp)

    def y_next(sign):
        return (lax.rem(y + NY + sign, NY) * NC + c, grp)

    def x_next(sign):
        return (rep, z * NX + lax.rem(x + NX + sign, NX))

    def z_peer(d):
        return lax.rem(z + d, NZ)

    barrier = pltpu.get_barrier_semaphore()

    def greet(d, _):
        pl.semaphore_signal(barrier, inc=1, device_id=(rep, peer(d)), device_id_type=MESH)
        return 0

    lax.fori_loop(1, GRP, greet, 0)
    for other in (sibling, y_next(1), y_next(-1)):
        pl.semaphore_signal(barrier, inc=1, device_id=other, device_id_type=MESH)
    pl.semaphore_wait(barrier, GRP + 2)

    def own_block(s):
        return pltpu.make_async_copy(
            ints.at[s, :, pl.ds(pl.multiple_of(grp * KB, KB), KB)],
            blocks.at[s, pl.ds(pl.multiple_of(grp * CB, CB), CB)],
            x_rsem.at[s],
        )

    def exchange(s):
        own_block(s).start()

        def send(d, _):
            to = peer(d)
            pltpu.make_async_remote_copy(
                ints.at[s, :, pl.ds(pl.multiple_of(to * KB, KB), KB)],
                blocks.at[s, pl.ds(pl.multiple_of(grp * CB, CB), CB)],
                x_ssem.at[s],
                x_rsem.at[s],
                device_id=(rep, to),
                device_id_type=MESH,
            ).start()
            return 0

        lax.fori_loop(1, GRP, send, 0)

    for s in range(AHEAD):
        exchange(s)

    def copy_1(s, ph, d):
        data, one, _, _, me, nxt = phases[ph]
        return pltpu.make_async_remote_copy(
            data.at[s, lax.rem(me + 2, 4), d],
            one.at[s, d],
            p_ssem.at[s, ph * 4 + d],
            p_rsem.at[s, ph * 4 + d],
            device_id=nxt(1 - 2 * d),
            device_id_type=MESH,
        )

    def copy_2(s, ph, d, h):
        data, _, two, _, me, nxt = phases[ph]
        return pltpu.make_async_remote_copy(
            data.at[s, lax.rem(me + (1, 3)[d], 4), h],
            two.at[s, d, h],
            p_ssem.at[s, ph * 4 + 2 + d],
            p_rsem.at[s, ph * 4 + 2 + d],
            device_id=nxt(1 - 2 * d),
            device_id_type=MESH,
        )

    def both_2(s, ph, d):
        _, _, two, _, _, nxt = phases[ph]
        return pltpu.make_async_remote_copy(
            two.at[s, d],
            two.at[s, d],
            p_ssem.at[s, ph * 4 + 2 + d],
            p_rsem.at[s, ph * 4 + 2 + d],
            device_id=nxt(1 - 2 * d),
            device_id_type=MESH,
        )

    phases = (
        (py_d, py_1, py_2, 64, y, y_next),
        (px_d, px_1, px_2, 16, x, x_next),
        (qx_d, qx_1, qx_2, 64, x, x_next),
        (qy_d, qy_1, qy_2, 16, y, y_next),
    )

    def begin(s, ph):
        for d in (0, 1):
            copy_1(s, ph, d).start()
        for d in (0, 1):
            copy_2(s, ph, d, 1 - d).start()

    def middle(s, ph):
        data, one, _, _, me, _ = phases[ph]
        for d in (0, 1):
            copy_1(s, ph, d).wait_recv()
            at = lax.rem(me + (1, 3)[d], 4)
            data[s, at, d] = data[s, at, d] + one[s, d]
            copy_2(s, ph, d, d).start()

    def end(s, ph):
        data, _, two, rows, me, _ = phases[ph]
        for d in (0, 1):
            both_2(s, ph, d).wait_recv()
        return data[s, me] + two[s, 0] + two[s, 1]

    def core_copy(s):
        return pltpu.make_async_remote_copy(
            c_send.at[s], c_recv.at[s], c_ssem.at[s], c_rsem.at[s], device_id=sibling, device_id_type=MESH
        )

    def prepare(s):
        low = (lax.broadcasted_iota(jnp.int32, (128, KB), 0) % 8) < 4

        def block(i, _):
            yy, cc = i // NC, lax.rem(i, NC)
            a = amps[s, pl.ds(pl.multiple_of(i * 128, 128), 128)]
            shape = (NZ // 2, 2, NX // 2, 8, KB)
            down = pltpu.roll(a, 4, 0)
            up = pltpu.roll(a, 124, 0)
            a5, d5, u5, l5 = (v.reshape(shape) for v in (a, down, up, low))
            even = jnp.where(l5[:, 0], a5[:, 0], d5[:, 1])
            odd = jnp.where(l5[:, 0], u5[:, 0], a5[:, 1])
            rows = jnp.concatenate(
                [v[:, p].reshape(NZ * R, KB) for p in range(NX // 2) for v in (even, odd)], axis=0
            )
            hi = rows.astype(jnp.bfloat16)
            lo = (rows - hi.astype(jnp.float32)).astype(jnp.bfloat16)
            lhs[pl.ds(pl.multiple_of(cc * HALF + yy * 128, 128), 128)] = jnp.concatenate([hi, lo], axis=1)
            return 0

        lax.fori_loop(0, NY * NC, block, 0)

    def product(half):
        left = lhs[pl.ds(pl.multiple_of(half * HALF, HALF), HALF)]
        dims = (((1,), (1,)), ((), ()))
        return lax.dot_general(left, rhs[0], dims, preferred_element_type=jnp.float32) + lax.dot_general(
            left, rhs[1], dims, preferred_element_type=jnp.float32
        )

    def multiply(s):
        pltpu.make_async_copy(blocks.at[s], blocks.at[s], x_rsem.at[s]).wait()
        k_index = first_k + lax.broadcasted_iota(jnp.int32, (COLS, KB), 1)
        b = jnp.where(k_index < k_count[s], blocks[s], 0.0)
        hi = b.astype(jnp.bfloat16)
        lo = (b - hi.astype(jnp.float32)).astype(jnp.bfloat16)
        rhs[0] = jnp.concatenate([hi, hi], axis=1)
        rhs[1] = jnp.concatenate([lo, lo], axis=1)
        c_send[s] = product(1 - c)
        core_copy(s).start()
        mine = product(c)
        core_copy(s).wait_recv()
        total = mine + c_recv[s]
        py_d[s] = total[:, :PC].reshape(NY, 2, 64, PC)
        q = total[:, PC:].reshape(NY, NX, NZ * R, QC)
        for xx in range(NX):
            qx_d[s, xx] = q[:, xx].reshape(2, 64, QC)
        begin(s, 0)
        begin(s, 2)

    def second(s):
        px_d[s] = end(s, 0).reshape(NX, 2, 16, PC)
        begin(s, 1)
        qy_d[s] = end(s, 2).reshape(NY, 2, 16, QC)
        begin(s, 3)

    def z_copy(p, d):
        to = z_peer(d)
        return pltpu.make_async_remote_copy(
            z_send.at[p, to],
            z_recv.at[p, z],
            z_ssem.at[p],
            z_rsem.at[p],
            device_id=(rep, to * NX + x),
            device_id_type=MESH,
        )

    def third(s):
        f = jnp.concatenate([end(s, 1).reshape(NZ * R, PC), end(s, 3).reshape(NZ * R, QC)], axis=1)

        @pl.when(lax.rem(s, 2) == 0)
        def _():
            f_even[...] = f

        @pl.when(lax.rem(s, 2) == 1)
        def _():
            p = s // 2
            e = f_even[...]
            low = (lax.broadcasted_iota(jnp.int32, f.shape, 0) % 8) < 4
            z_even = jnp.where(low, e, pltpu.roll(f, 4, 0)).reshape(NZ // 2, 8, COLS)
            z_odd = jnp.where(low, pltpu.roll(e, NZ * R - 4, 0), f).reshape(NZ // 2, 8, COLS)
            for i in range(NZ // 2):
                z_send[p, 2 * i] = z_even[i]
                z_send[p, 2 * i + 1] = z_odd[i]
            pltpu.make_async_copy(z_send.at[p, z], z_recv.at[p, z], z_rsem.at[p]).start()
            for d in range(1, NZ):
                z_copy(p, d).start()

    def step(t, _):
        @pl.when(t < NIRR)
        def _():
            prepare(t)

        @pl.when(t + AHEAD < NIRR)
        def _():
            exchange(t + AHEAD)

        @pl.when((t >= 1) & (t < NIRR + 1))
        def _():
            middle(t - 1, 0)
            middle(t - 1, 2)

        @pl.when(t >= 3)
        def _():
            third(t - 3)

        @pl.when((t >= 2) & (t < NIRR + 2))
        def _():
            second(t - 2)

        @pl.when(t < NIRR)
        def _():
            multiply(t)

        @pl.when((t >= 2) & (t < NIRR + 2))
        def _():
            middle(t - 2, 1)
            middle(t - 2, 3)

        return 0

    lax.fori_loop(0, NIRR + 3, step, 0)

    for p in range(NIRR // 2):
        pltpu.make_async_copy(z_recv.at[p], z_recv.at[p], z_rsem.at[p]).wait()
        total = z_recv[p, 0]
        for i in range(1, NZ):
            total = total + z_recv[p, i]
        out[p] = total

    def drain(s, _):
        most = blocks.at[s, pl.ds(0, COLS - CB)]
        pltpu.make_async_copy(most, most, x_ssem.at[s]).wait()
        core_copy(s).wait_send()
        for ph in range(4):
            for d in (0, 1):
                copy_1(s, ph, d).wait_send()
                both_2(s, ph, d).wait_send()
        return 0

    lax.fori_loop(0, NIRR, drain, 0)
    for p in range(NIRR // 2):
        most = z_send.at[p, pl.ds(0, NZ - 1)]
        pltpu.make_async_copy(most, most, z_ssem.at[p]).wait()


def cycle_of(amps, ints, k_count):
    f32 = jnp.float32
    return pl.pallas_call(
        kernel,
        out_shape=jax.ShapeDtypeStruct((NIRR // 2, 2 * R, COLS), f32),
        in_specs=[
            pl.BlockSpec(memory_space=pltpu.VMEM),
            pl.BlockSpec(memory_space=pl.ANY),
            pl.BlockSpec(memory_space=pltpu.SMEM),
        ],
        out_specs=pl.BlockSpec(memory_space=pltpu.VMEM),
        scratch_shapes=[
            pltpu.VMEM((NIRR, COLS, KB), f32),
            pltpu.VMEM((ROWS, 2 * KB), jnp.bfloat16),
            pltpu.VMEM((2, COLS, 2 * KB), jnp.bfloat16),
            pltpu.VMEM((NIRR, HALF, COLS), f32),
            pltpu.VMEM((NIRR, HALF, COLS), f32),
            pltpu.VMEM((NIRR, 4, 2, 64, PC), f32),
            pltpu.VMEM((NIRR, 2, 64, PC), f32),
            pltpu.VMEM((NIRR, 2, 2, 64, PC), f32),
            pltpu.VMEM((NIRR, 4, 2, 16, PC), f32),
            pltpu.VMEM((NIRR, 2, 16, PC), f32),
            pltpu.VMEM((NIRR, 2, 2, 16, PC), f32),
            pltpu.VMEM((NIRR, 4, 2, 64, QC), f32),
            pltpu.VMEM((NIRR, 2, 64, QC), f32),
            pltpu.VMEM((NIRR, 2, 2, 64, QC), f32),
            pltpu.VMEM((NIRR, 4, 2, 16, QC), f32),
            pltpu.VMEM((NIRR, 2, 16, QC), f32),
            pltpu.VMEM((NIRR, 2, 2, 16, QC), f32),
            pltpu.VMEM((NZ * R, COLS), f32),
            pltpu.VMEM((NIRR // 2, NZ, 2 * R, COLS), f32),
            pltpu.VMEM((NIRR // 2, NZ, 2 * R, COLS), f32),
            pltpu.SemaphoreType.DMA((NIRR,)),
            pltpu.SemaphoreType.DMA((NIRR,)),
            pltpu.SemaphoreType.DMA((NIRR,)),
            pltpu.SemaphoreType.DMA((NIRR,)),
            pltpu.SemaphoreType.DMA((NIRR, 16)),
            pltpu.SemaphoreType.DMA((NIRR, 16)),
            pltpu.SemaphoreType.DMA((NIRR // 2,)),
            pltpu.SemaphoreType.DMA((NIRR // 2,)),
        ],
        compiler_params=pltpu.CompilerParams(
            collective_id=0, has_side_effects=True, vmem_limit_bytes=56 * 2**20
        ),
        cost_estimate=pl.CostEstimate(
            flops=2 * NIRR * ROWS * COLS * KB * 4, bytes_accessed=6 * 2**20, transcendentals=0
        ),
    )(amps, ints, k_count)


def local(amps, integrals, residual_other, row_gap, col_gap, row_count, k_count, col_count):
    position = lax.axis_index("rep") * lax.axis_size("grp") + lax.axis_index("grp")
    rows_here = residual_other.shape[0]
    first_row = position * rows_here
    cycle = cycle_of(amps, jnp.swapaxes(integrals, 1, 2), k_count)
    cycle_sum = jnp.swapaxes(cycle.reshape(NIRR, R, COLS), 0, 1)
    row_index = first_row + jnp.arange(rows_here, dtype=jnp.int32)[:, None, None]
    col_index = jnp.arange(col_gap.shape[1], dtype=jnp.int32)[None, None, :]
    live_mask = (row_index < row_count[None, :, None]) & (col_index < col_count[None, :, None])
    denominator = row_gap[:, :, None] + col_gap[None, :, :]
    return jnp.where(live_mask, -(cycle_sum + residual_other) / denominator, 0.0)


def solution(mesh):
    return jax.shard_map(
        local,
        mesh=mesh,
        in_specs=(
            P(None, None, ("rep", "grp")),
            P(None, "rep", "grp"),
            P(("rep", "grp"), None, None),
            P(("rep", "grp"), None),
            P(),
            P(),
            P(),
            P(),
        ),
        out_specs=P(("rep", "grp"), None, None),
        check_vma=False,
    )
```

```python
import jax
import jax.numpy as jnp
from jax import lax
from jax.experimental import pallas as pl
from jax.experimental.pallas import tpu as pltpu
from jax.sharding import PartitionSpec as P

MESH = pl.DeviceIdType.MESH
NY, NC, NZ, NX = 4, 2, 8, 4
GRP = NZ * NX
NIRR = 8
ROWS = 1024
COLS = 512
KB = 128
R = 4
HALF = ROWS // NC
NST = 2 * NIRR
CB = 8
WIDE = GRP * CB
LANES = 128
UNITS = NZ * R * (WIDE // LANES)
PR = 40
QR = UNITS - PR
AHEAD = 6
LAG_M, LAG_S, LAG_T, LAG_Z = 2, 4, 6, 8


def kernel(
    amps, ints, residual, col_gap, row_gap, row_count, k_count, col_count, out,
    left, blocks, lhs, rhs, c_send, c_recv, c_mine,
    py_d, py_1, py_2, px_d, px_r,
    qx_d, qx_1, qx_2, qy_d, qy_r,
    f_even, z_send, z_recv, gaps, limits, cycle,
    a_sem, x_ssem, x_rsem, c_ssem, c_rsem, p_ssem, p_rsem, d_ssem, d_rsem, z_ssem, z_rsem,
):
    rep, grp = lax.axis_index("rep"), lax.axis_index("grp")
    y, c = rep // NC, rep % NC
    z, x = grp // NX, grp % NX
    first_k = (rep * GRP + grp) * KB

    def swing(j, n):
        step = (j + 1) // 2
        return lax.rem(n // 2 + n + (1 - 2 * lax.rem(j, 2)) * step, n)

    def peer(d):
        return lax.rem(z + swing(d // NX, NZ), NZ) * NX + lax.rem(x + swing(lax.rem(d, NX), NX), NX)

    sibling = (y * NC + 1 - c, grp)

    def y_next(sign):
        return (lax.rem(y + sign, NY) * NC + c, grp)

    def x_next(sign):
        return (rep, z * NX + lax.rem(x + sign, NX))

    def z_peer(d):
        return lax.rem(z + d, NZ)

    def load(s):
        return pltpu.make_async_copy(amps.at[s], left.at[s], a_sem.at[s])

    for s in range(NIRR):
        load(s).start()
    barrier = pltpu.get_barrier_semaphore()

    def greet(d, _):
        pl.semaphore_signal(barrier, inc=1, device_id=(rep, peer(d)), device_id_type=MESH)
        return 0

    lax.fori_loop(0, GRP - 1, greet, 0)
    for other in (sibling, y_next(1), y_next(2), y_next(3)):
        pl.semaphore_signal(barrier, inc=1, device_id=other, device_id_type=MESH)

    def own_block(s):
        return pltpu.make_async_copy(
            ints.at[s // 2, lax.rem(s, 2), :, pl.ds(pl.multiple_of(grp * KB, KB), KB)],
            blocks.at[s, pl.ds(pl.multiple_of(grp * CB, CB), CB)],
            x_rsem.at[s],
        )

    def exchange(s):
        own_block(s).start()

        def send(d, _):
            to = peer(d)
            pltpu.make_async_remote_copy(
                ints.at[s // 2, lax.rem(s, 2), :, pl.ds(pl.multiple_of(to * KB, KB), KB)],
                blocks.at[s, pl.ds(pl.multiple_of(grp * CB, CB), CB)],
                x_ssem.at[s],
                x_rsem.at[s],
                device_id=(rep, to),
                device_id_type=MESH,
            ).start()
            return 0

        lax.fori_loop(0, GRP - 1, send, 0)

    def copy_1(s, ph, d):
        data, one, _, me, nxt = phases[ph]
        return pltpu.make_async_remote_copy(
            data.at[s, lax.rem(me + 2, 4), d],
            one.at[s, d],
            p_ssem.at[s, ph * 4 + d],
            p_rsem.at[s, ph * 4 + d],
            device_id=nxt(1 + 2 * d),
            device_id_type=MESH,
        )

    def copy_2(s, ph, d, h):
        data, _, two, me, nxt = phases[ph]
        return pltpu.make_async_remote_copy(
            data.at[s, lax.rem(me + (1, 3)[d], 4), h],
            two.at[s, d, h],
            p_ssem.at[s, ph * 4 + 2 + d],
            p_rsem.at[s, ph * 4 + 2 + d],
            device_id=nxt(1 + 2 * d),
            device_id_type=MESH,
        )

    def both_2(s, ph, d):
        _, _, two, _, nxt = phases[ph]
        return pltpu.make_async_remote_copy(
            two.at[s, d],
            two.at[s, d],
            p_ssem.at[s, ph * 4 + 2 + d],
            p_rsem.at[s, ph * 4 + 2 + d],
            device_id=nxt(1 + 2 * d),
            device_id_type=MESH,
        )

    phases = (
        (py_d, py_1, py_2, y, y_next),
        (qx_d, qx_1, qx_2, x, x_next),
    )

    def begin(s, ph):
        for d in (0, 1):
            copy_1(s, ph, d).start()
        for d in (0, 1):
            copy_2(s, ph, d, 1 - d).start()

    def middle(s, ph):
        data, one, _, me, _ = phases[ph]
        for d in (0, 1):
            copy_1(s, ph, d).wait_recv()
            at = lax.rem(me + (1, 3)[d], 4)
            data[s, at, d] = data[s, at, d] + one[s, d]
            copy_2(s, ph, d, d).start()

    def end(s, ph):
        data, _, two, me, _ = phases[ph]
        for d in (0, 1):
            both_2(s, ph, d).wait_recv()
        return data[s, me] + two[s, 0] + two[s, 1]

    straight = ((px_d, px_r, x, x_next), (qy_d, qy_r, y, y_next))

    def copy_straight(s, ph, d):
        data, got, me, nxt = straight[ph]
        return pltpu.make_async_remote_copy(
            data.at[s, lax.rem(me + d, 4)],
            got.at[s, d - 1],
            d_ssem.at[s, ph * 3 + d - 1],
            d_rsem.at[s, ph * 3 + d - 1],
            device_id=nxt(d),
            device_id_type=MESH,
        )

    def begin_straight(s, ph):
        for d in (2, 1, 3):
            copy_straight(s, ph, d).start()

    def end_straight(s, ph):
        data, got, me, _ = straight[ph]
        for d in (1, 2, 3):
            copy_straight(s, ph, d).wait_recv()
        return data[s, me] + got[s, 0] + got[s, 1] + got[s, 2]

    def core_copy(s):
        return pltpu.make_async_remote_copy(
            c_send.at[s], c_recv.at[s], c_ssem.at[s], c_rsem.at[s], device_id=sibling, device_id_type=MESH
        )

    def prepare(s):
        load(s).wait()
        low = (lax.broadcasted_iota(jnp.int32, (128, KB), 0) % 8) < 4

        def block(i, _):
            yy, cc = i // NC, lax.rem(i, NC)
            a = left[s, pl.ds(pl.multiple_of(i * 128, 128), 128)]
            shape = (NZ // 2, 2, NX // 2, 8, KB)
            down = pltpu.roll(a, 4, 0)
            up = pltpu.roll(a, 124, 0)
            a5, d5, u5, l5 = (v.reshape(shape) for v in (a, down, up, low))
            even = jnp.where(l5[:, 0], a5[:, 0], d5[:, 1])
            odd = jnp.where(l5[:, 0], u5[:, 0], a5[:, 1])
            rows = jnp.concatenate(
                [v[:, p].reshape(NZ * R, KB) for p in range(NX // 2) for v in (even, odd)], axis=0
            )
            hi = rows.astype(jnp.bfloat16)
            lo = (rows - hi.astype(jnp.float32)).astype(jnp.bfloat16)
            lhs[pl.ds(pl.multiple_of(cc * HALF + yy * 128, 128), 128)] = jnp.concatenate([hi, lo], axis=1)
            return 0

        lax.fori_loop(0, NY * NC, block, 0)

    def product(half):
        rows = lhs[pl.ds(pl.multiple_of(half * HALF, HALF), HALF)]
        dims = (((1,), (1,)), ((), ()))
        return lax.dot_general(rows, rhs[0], dims, preferred_element_type=jnp.float32) + lax.dot_general(
            rows, rhs[1], dims, preferred_element_type=jnp.float32
        )

    def multiply(s):
        pltpu.make_async_copy(blocks.at[s], blocks.at[s], x_rsem.at[s]).wait()
        k_index = first_k + lax.broadcasted_iota(jnp.int32, (WIDE, KB), 1)
        b = jnp.where(k_index < k_count[s // 2], blocks[s], 0.0)
        hi = b.astype(jnp.bfloat16)
        lo = (b - hi.astype(jnp.float32)).astype(jnp.bfloat16)
        rhs[0] = jnp.concatenate([hi, hi], axis=1)
        rhs[1] = jnp.concatenate([lo, lo], axis=1)
        c_send[s] = product(1 - c)
        core_copy(s).start()
        c_mine[...] = product(c)

    def first(s):
        core_copy(s).wait_recv()
        total = (c_mine[...] + c_recv[s]).reshape(NY, NX, NZ * R, WIDE)
        total = jnp.concatenate([total[..., :LANES], total[..., LANES:]], axis=2)
        py_d[s] = total[:, :, :PR].reshape(NY, 2, NX * PR // 2, LANES)
        begin(s, 0)
        for xx in range(NX):
            qx_d[s, xx] = total[:, xx, PR:].reshape(2, NY * QR // 2, LANES)
        begin(s, 1)

    def second(s):
        px_d[s] = end(s, 0).reshape(NX, PR, LANES)
        begin_straight(s, 0)
        qy_d[s] = end(s, 1).reshape(NY, QR, LANES)
        begin_straight(s, 1)

    def z_copy(p, d):
        to = z_peer(d)
        return pltpu.make_async_remote_copy(
            z_send.at[p, to],
            z_recv.at[p, z],
            z_ssem.at[p],
            z_rsem.at[p],
            device_id=(rep, to * NX + x),
            device_id_type=MESH,
        )

    def third(s):
        f = jnp.concatenate([end_straight(s, 0), end_straight(s, 1)], axis=0)
        f = jnp.concatenate([f[: NZ * R], f[NZ * R :]], axis=1)

        @pl.when(lax.rem(s, 2) == 0)
        def _():
            f_even[...] = f

        @pl.when(lax.rem(s, 2) == 1)
        def _():
            p = s // 2
            e = f_even[...]
            low = (lax.broadcasted_iota(jnp.int32, f.shape, 0) % 8) < 4
            z_even = jnp.where(low, e, pltpu.roll(f, 4, 0)).reshape(NZ // 2, 8, WIDE)
            z_odd = jnp.where(low, pltpu.roll(e, NZ * R - 4, 0), f).reshape(NZ // 2, 8, WIDE)
            for i in range(NZ // 2):
                z_send[p, 2 * i] = z_even[i]
                z_send[p, 2 * i + 1] = z_odd[i]
            pltpu.make_async_copy(z_send.at[p, z], z_recv.at[p, z], z_rsem.at[p]).start()
            for d in (4, 3, 5, 2, 6, 1, 7):
                z_copy(p, d).start()

    def last(p):
        pltpu.make_async_copy(z_recv.at[p], z_recv.at[p], z_rsem.at[p]).wait()
        total = z_recv[p, 0]
        for i in range(1, NZ):
            total = total + z_recv[p, i]
        for i in range(2 * R):
            cycle[i // R, i % R, pl.ds(p, 1)] = total[i : i + 1]

    first_row = (rep * GRP + grp) * R
    irrep = lax.broadcasted_iota(jnp.int32, (NIRR, COLS), 0)
    for r in range(R):
        gap = jnp.zeros((NIRR, COLS), jnp.float32)
        limit = jnp.zeros((NIRR, COLS), jnp.int32)
        for s in range(NIRR):
            gap = jnp.where(irrep == s, row_gap[r, s], gap)
            limit = jnp.where(irrep == s, jnp.where(first_row + r < row_count[s], col_count[s], 0), limit)
        gaps[r] = gap + col_gap[...]
        limits[r] = limit

    prepare(0)
    pl.semaphore_wait(barrier, GRP + 3)
    for s in range(AHEAD):
        exchange(s)

    def step(t, _):
        @pl.when(t + AHEAD < NST)
        def _():
            exchange(t + AHEAD)

        @pl.when(t < NST)
        def _():
            multiply(t)

        @pl.when((t >= LAG_M) & (t < NST + LAG_M))
        def _():
            middle(t - LAG_M, 0)
            middle(t - LAG_M, 1)

        @pl.when((t >= LAG_S) & (t < NST + LAG_S))
        def _():
            second(t - LAG_S)

        @pl.when((t >= LAG_T) & (t < NST + LAG_T))
        def _():
            third(t - LAG_T)

        @pl.when((t < NST - 1) & (lax.rem(t, 2) == 1))
        def _():
            prepare((t + 1) // 2)

        @pl.when(t < NST)
        def _():
            first(t)

        @pl.when((t >= LAG_Z) & (lax.rem(t - LAG_Z, 2) == 1))
        def _():
            last((t - LAG_Z) // 2)

        return 0

    lax.fori_loop(0, NST + LAG_Z, step, 0)

    lane = lax.broadcasted_iota(jnp.int32, (NIRR, 128), 1)
    for r in range(R):
        for q in range(COLS // 128):
            total = jnp.zeros((NIRR, 128), jnp.float32)
            for h in range(2):
                part = cycle[h, r, :, 128 * (q // 2) : 128 * (q // 2) + 128]
                for g in range(8):
                    at = 16 * g + CB * h
                    moved = pltpu.roll(part, (at - 64 * (q % 2) - CB * g) % 128, 1)
                    total = jnp.where((lane >= at) & (lane < at + CB), moved, total)
            here = slice(128 * q, 128 * q + 128)
            value = -(total + residual[r, :, here]) / gaps[r, :, here]
            out[r, :, here] = jnp.where(lane + 128 * q < limits[r, :, here], value, 0.0)

    def drain(s, _):
        most = blocks.at[s, pl.ds(0, WIDE - CB)]
        pltpu.make_async_copy(most, most, x_ssem.at[s]).wait()
        core_copy(s).wait_send()
        for ph in range(2):
            for d in (0, 1):
                copy_1(s, ph, d).wait_send()
                both_2(s, ph, d).wait_send()
            for d in (1, 2, 3):
                copy_straight(s, ph, d).wait_send()
        return 0

    lax.fori_loop(0, NST, drain, 0)
    for p in range(NIRR):
        most = z_send.at[p, pl.ds(0, NZ - 1)]
        pltpu.make_async_copy(most, most, z_ssem.at[p]).wait()


def local(amps, integrals, residual_other, row_gap, col_gap, row_count, k_count, col_count):
    f32 = jnp.float32
    vmem, smem = pl.BlockSpec(memory_space=pltpu.VMEM), pl.BlockSpec(memory_space=pltpu.SMEM)
    return pl.pallas_call(
        kernel,
        out_shape=jax.ShapeDtypeStruct((R, NIRR, COLS), f32),
        in_specs=[pl.BlockSpec(memory_space=pl.ANY), pl.BlockSpec(memory_space=pl.ANY), vmem, vmem, smem, smem, smem, smem],
        out_specs=vmem,
        scratch_shapes=[
            pltpu.VMEM((NIRR, ROWS, KB), f32),
            pltpu.VMEM((NST, WIDE, KB), f32),
            pltpu.VMEM((ROWS, 2 * KB), jnp.bfloat16),
            pltpu.VMEM((2, WIDE, 2 * KB), jnp.bfloat16),
            pltpu.VMEM((NST, HALF, WIDE), f32),
            pltpu.VMEM((NST, HALF, WIDE), f32),
            pltpu.VMEM((HALF, WIDE), f32),
            pltpu.VMEM((NST, 4, 2, NX * PR // 2, LANES), f32),
            pltpu.VMEM((NST, 2, NX * PR // 2, LANES), f32),
            pltpu.VMEM((NST, 2, 2, NX * PR // 2, LANES), f32),
            pltpu.VMEM((NST, NX, PR, LANES), f32),
            pltpu.VMEM((NST, 3, PR, LANES), f32),
            pltpu.VMEM((NST, 4, 2, NY * QR // 2, LANES), f32),
            pltpu.VMEM((NST, 2, NY * QR // 2, LANES), f32),
            pltpu.VMEM((NST, 2, 2, NY * QR // 2, LANES), f32),
            pltpu.VMEM((NST, NY, QR, LANES), f32),
            pltpu.VMEM((NST, 3, QR, LANES), f32),
            pltpu.VMEM((NZ * R, WIDE), f32),
            pltpu.VMEM((NIRR, NZ, 2 * R, WIDE), f32),
            pltpu.VMEM((NIRR, NZ, 2 * R, WIDE), f32),
            pltpu.VMEM((R, NIRR, COLS), f32),
            pltpu.VMEM((R, NIRR, COLS), jnp.int32),
            pltpu.VMEM((2, R, NIRR, WIDE), f32),
            pltpu.SemaphoreType.DMA((NIRR,)),
            pltpu.SemaphoreType.DMA((NST,)),
            pltpu.SemaphoreType.DMA((NST,)),
            pltpu.SemaphoreType.DMA((NST,)),
            pltpu.SemaphoreType.DMA((NST,)),
            pltpu.SemaphoreType.DMA((NST, 8)),
            pltpu.SemaphoreType.DMA((NST, 8)),
            pltpu.SemaphoreType.DMA((NST, 6)),
            pltpu.SemaphoreType.DMA((NST, 6)),
            pltpu.SemaphoreType.DMA((NIRR,)),
            pltpu.SemaphoreType.DMA((NIRR,)),
        ],
        compiler_params=pltpu.CompilerParams(
            collective_id=0, has_side_effects=True, vmem_limit_bytes=56 * 2**20
        ),
        cost_estimate=pl.CostEstimate(
            flops=2 * NIRR * ROWS * COLS * KB * 4, bytes_accessed=6 * 2**20, transcendentals=0
        ),
    )(amps, jnp.swapaxes(integrals, 1, 2).reshape(NIRR, 2, CB, -1), residual_other, col_gap, row_gap, row_count, k_count, col_count)


def solution(mesh):
    return jax.shard_map(
        local,
        mesh=mesh,
        in_specs=(
            P(None, None, ("rep", "grp")),
            P(None, "rep", "grp"),
            P(("rep", "grp"), None, None),
            P(("rep", "grp"), None),
            P(),
            P(),
            P(),
            P(),
        ),
        out_specs=P(("rep", "grp"), None, None),
        check_vma=False,
    )
```

```python
import jax
import jax.numpy as jnp
from jax import lax
from jax.experimental import pallas as pl
from jax.experimental.pallas import tpu as pltpu
from jax.sharding import PartitionSpec as P

MESH = pl.DeviceIdType.MESH
NY, NC, NZ, NX = 4, 2, 8, 4
GRP = NZ * NX
NIRR = 8
ROWS = 1024
COLS = 512
KB = 128
R = 4
HALF = ROWS // NC
NST = 2 * NIRR
CB = 8
WIDE = GRP * CB
LANES = 128
UNITS = NZ * R * (WIDE // LANES)
PR = 48
QR = UNITS - PR
AHEAD = 6
LAG_M, LAG_S, LAG_T = 2, 4, 6
HELD = (NST - LAG_T) // 2


def kernel(
    amps, ints, residual_in, col_gap_in, row_gap, row_count, k_count, col_count, out,
    residual, col_gap, left, blocks, lhs, rhs, c_send, c_recv, c_mine,
    py_d, py_1, py_2, px_d, px_r,
    qx_d, qx_1, qx_2, qy_d, qy_r,
    f_even, z_send, z_recv, gaps, limits, cycle,
    i_sem, a_sem, x_ssem, x_rsem, c_ssem, c_rsem, p_ssem, p_rsem, d_ssem, d_rsem, z_ssem, z_rsem,
):
    rep, grp = lax.axis_index("rep"), lax.axis_index("grp")
    y, c = rep // NC, rep % NC
    z, x = grp // NX, grp % NX
    first_k = (rep * GRP + grp) * KB

    def swing(j, n):
        step = (j + 1) // 2
        return lax.rem(n // 2 + n + (1 - 2 * lax.rem(j, 2)) * step, n)

    def peer(d):
        return lax.rem(z + swing(d // NX, NZ), NZ) * NX + lax.rem(x + swing(lax.rem(d, NX), NX), NX)

    sibling = (y * NC + 1 - c, grp)

    def y_next(sign):
        return (lax.rem(y + sign, NY) * NC + c, grp)

    def x_next(sign):
        return (rep, z * NX + lax.rem(x + sign, NX))

    def z_peer(d):
        return lax.rem(z + d, NZ)

    def load(s):
        return pltpu.make_async_copy(amps.at[s], left.at[s], a_sem.at[s])

    for s in range(NIRR):
        load(s).start()
    inputs = (
        pltpu.make_async_copy(col_gap_in, col_gap, i_sem.at[0]),
        pltpu.make_async_copy(residual_in, residual, i_sem.at[1]),
    )
    for copy in inputs:
        copy.start()
    barrier = pltpu.get_barrier_semaphore()

    def greet(d, _):
        pl.semaphore_signal(barrier, inc=1, device_id=(rep, peer(d)), device_id_type=MESH)
        return 0

    lax.fori_loop(0, GRP - 1, greet, 0)
    for other in (sibling, y_next(1), y_next(2), y_next(3)):
        pl.semaphore_signal(barrier, inc=1, device_id=other, device_id_type=MESH)

    def own_block(s):
        return pltpu.make_async_copy(
            ints.at[s // 2, lax.rem(s, 2), :, pl.ds(pl.multiple_of(grp * KB, KB), KB)],
            blocks.at[s, pl.ds(pl.multiple_of(grp * CB, CB), CB)],
            x_rsem.at[s],
        )

    def exchange(s):
        own_block(s).start()

        def send(d, _):
            to = peer(d)
            pltpu.make_async_remote_copy(
                ints.at[s // 2, lax.rem(s, 2), :, pl.ds(pl.multiple_of(to * KB, KB), KB)],
                blocks.at[s, pl.ds(pl.multiple_of(grp * CB, CB), CB)],
                x_ssem.at[s],
                x_rsem.at[s],
                device_id=(rep, to),
                device_id_type=MESH,
            ).start()
            return 0

        lax.fori_loop(0, GRP - 1, send, 0)

    def copy_1(s, ph, d):
        data, one, _, me, nxt = phases[ph]
        return pltpu.make_async_remote_copy(
            data.at[s, lax.rem(me + 2, 4), d],
            one.at[s, d],
            p_ssem.at[s, ph * 4 + d],
            p_rsem.at[s, ph * 4 + d],
            device_id=nxt(1 + 2 * d),
            device_id_type=MESH,
        )

    def copy_2(s, ph, d, h):
        data, _, two, me, nxt = phases[ph]
        return pltpu.make_async_remote_copy(
            data.at[s, lax.rem(me + (1, 3)[d], 4), h],
            two.at[s, d, h],
            p_ssem.at[s, ph * 4 + 2 + d],
            p_rsem.at[s, ph * 4 + 2 + d],
            device_id=nxt(1 + 2 * d),
            device_id_type=MESH,
        )

    def both_2(s, ph, d):
        _, _, two, _, nxt = phases[ph]
        return pltpu.make_async_remote_copy(
            two.at[s, d],
            two.at[s, d],
            p_ssem.at[s, ph * 4 + 2 + d],
            p_rsem.at[s, ph * 4 + 2 + d],
            device_id=nxt(1 + 2 * d),
            device_id_type=MESH,
        )

    phases = (
        (py_d, py_1, py_2, y, y_next),
        (qx_d, qx_1, qx_2, x, x_next),
    )

    def begin(s, ph):
        for d in (0, 1):
            copy_1(s, ph, d).start()
        for d in (0, 1):
            copy_2(s, ph, d, 1 - d).start()

    def middle(s, ph):
        data, one, _, me, _ = phases[ph]
        for d in (0, 1):
            copy_1(s, ph, d).wait_recv()
            at = lax.rem(me + (1, 3)[d], 4)
            data[s, at, d] = data[s, at, d] + one[s, d]
            copy_2(s, ph, d, d).start()

    def end(s, ph):
        data, _, two, me, _ = phases[ph]
        for d in (0, 1):
            both_2(s, ph, d).wait_recv()
        return data[s, me] + two[s, 0] + two[s, 1]

    straight = ((px_d, px_r, x, x_next), (qy_d, qy_r, y, y_next))

    def copy_straight(s, ph, d):
        data, got, me, nxt = straight[ph]
        return pltpu.make_async_remote_copy(
            data.at[s, lax.rem(me + d, 4)],
            got.at[s, d - 1],
            d_ssem.at[s, ph * 3 + d - 1],
            d_rsem.at[s, ph * 3 + d - 1],
            device_id=nxt(d),
            device_id_type=MESH,
        )

    def begin_straight(s, ph):
        for d in (2, 1, 3):
            copy_straight(s, ph, d).start()

    def end_straight(s, ph):
        data, got, me, _ = straight[ph]
        for d in (1, 2, 3):
            copy_straight(s, ph, d).wait_recv()
        return data[s, me] + got[s, 0] + got[s, 1] + got[s, 2]

    def core_copy(s):
        return pltpu.make_async_remote_copy(
            c_send.at[s], c_recv.at[s], c_ssem.at[s], c_rsem.at[s], device_id=sibling, device_id_type=MESH
        )

    def prepare(s):
        load(s).wait()
        low = (lax.broadcasted_iota(jnp.int32, (128, KB), 0) % 8) < 4

        def block(i, _):
            yy, cc = i // NC, lax.rem(i, NC)
            a = left[s, pl.ds(pl.multiple_of(i * 128, 128), 128)]
            shape = (NZ // 2, 2, NX // 2, 8, KB)
            down = pltpu.roll(a, 4, 0)
            up = pltpu.roll(a, 124, 0)
            a5, d5, u5, l5 = (v.reshape(shape) for v in (a, down, up, low))
            even = jnp.where(l5[:, 0], a5[:, 0], d5[:, 1])
            odd = jnp.where(l5[:, 0], u5[:, 0], a5[:, 1])
            rows = jnp.concatenate(
                [v[:, p].reshape(NZ * R, KB) for p in range(NX // 2) for v in (even, odd)], axis=0
            )
            hi = rows.astype(jnp.bfloat16)
            lo = (rows - hi.astype(jnp.float32)).astype(jnp.bfloat16)
            lhs[pl.ds(pl.multiple_of(cc * HALF + yy * 128, 128), 128)] = jnp.concatenate([hi, lo], axis=1)
            return 0

        lax.fori_loop(0, NY * NC, block, 0)

    def product(half):
        rows = lhs[pl.ds(pl.multiple_of(half * HALF, HALF), HALF)]
        dims = (((1,), (1,)), ((), ()))
        return lax.dot_general(rows, rhs[0], dims, preferred_element_type=jnp.float32) + lax.dot_general(
            rows, rhs[1], dims, preferred_element_type=jnp.float32
        )

    def multiply(s):
        pltpu.make_async_copy(blocks.at[s], blocks.at[s], x_rsem.at[s]).wait()
        k_index = first_k + lax.broadcasted_iota(jnp.int32, (WIDE, KB), 1)
        b = jnp.where(k_index < k_count[s // 2], blocks[s], 0.0)
        hi = b.astype(jnp.bfloat16)
        lo = (b - hi.astype(jnp.float32)).astype(jnp.bfloat16)
        rhs[0] = jnp.concatenate([hi, hi], axis=1)
        rhs[1] = jnp.concatenate([lo, lo], axis=1)
        c_send[s] = product(1 - c)
        core_copy(s).start()
        c_mine[...] = product(c)

    def first(s):
        core_copy(s).wait_recv()
        total = (c_mine[...] + c_recv[s]).reshape(NY, NX, NZ * R, WIDE)
        total = jnp.concatenate([total[..., :LANES], total[..., LANES:]], axis=2)
        py_d[s] = total[:, :, :PR].reshape(NY, 2, NX * PR // 2, LANES)
        begin(s, 0)
        for xx in range(NX):
            qx_d[s, xx] = total[:, xx, PR:].reshape(2, NY * QR // 2, LANES)
        begin(s, 1)

    def second(s):
        px_d[s] = end(s, 0).reshape(NX, PR, LANES)
        begin_straight(s, 0)
        qy_d[s] = end(s, 1).reshape(NY, QR, LANES)
        begin_straight(s, 1)

    def z_copy(p, d):
        to = z_peer(d)
        return pltpu.make_async_remote_copy(
            z_send.at[p, to],
            z_recv.at[p, z],
            z_ssem.at[p],
            z_rsem.at[p],
            device_id=(rep, to * NX + x),
            device_id_type=MESH,
        )

    def third(s):
        f = jnp.concatenate([end_straight(s, 0), end_straight(s, 1)], axis=0)
        f = jnp.concatenate([f[: NZ * R], f[NZ * R :]], axis=1)

        @pl.when(lax.rem(s, 2) == 0)
        def _():
            f_even[...] = f

        @pl.when(lax.rem(s, 2) == 1)
        def _():
            p = s // 2
            e = f_even[...]
            low = (lax.broadcasted_iota(jnp.int32, f.shape, 0) % 8) < 4
            z_even = jnp.where(low, e, pltpu.roll(f, 4, 0)).reshape(NZ // 2, 8, WIDE)
            z_odd = jnp.where(low, pltpu.roll(e, NZ * R - 4, 0), f).reshape(NZ // 2, 8, WIDE)
            for i in range(NZ // 2):
                z_send[p, 2 * i] = z_even[i]
                z_send[p, 2 * i + 1] = z_odd[i]

    def spread(p):
        pltpu.make_async_copy(z_send.at[p, z], z_recv.at[p, z], z_rsem.at[p]).start()
        for d in (4, 3, 5, 2, 6, 1, 7):
            z_copy(p, d).start()

    lane = lax.broadcasted_iota(jnp.int32, (2 * R, LANES), 1)

    def last(p):
        pltpu.make_async_copy(z_recv.at[p], z_recv.at[p], z_rsem.at[p]).wait()
        total = z_recv[p, 0]
        for i in range(1, NZ):
            total = total + z_recv[p, i]
        for q in range(COLS // LANES):
            part = total[:, LANES * (q // 2) : LANES * (q // 2 + 1)]
            both = jnp.zeros((2 * R, LANES), jnp.float32)
            for k in range(9):
                moved = pltpu.roll(part, (CB * k - 64 * (q % 2)) % LANES, 1)
                both = jnp.where((lane >= 16 * k - CB) & (lane < 16 * k + CB), moved, both)
            rows = jnp.where(lane % 16 < CB, both, pltpu.roll(both, R, 0))
            for r in range(R):
                cycle[r, p : p + 1, LANES * q : LANES * (q + 1)] = rows[r : r + 1]

    for copy in inputs:
        copy.wait()
    first_row = (rep * GRP + grp) * R
    irrep = lax.broadcasted_iota(jnp.int32, (NIRR, COLS), 0)
    for r in range(R):
        gap = jnp.zeros((NIRR, COLS), jnp.float32)
        limit = jnp.zeros((NIRR, COLS), jnp.int32)
        for s in range(NIRR):
            gap = jnp.where(irrep == s, row_gap[r, s], gap)
            limit = jnp.where(irrep == s, jnp.where(first_row + r < row_count[s], col_count[s], 0), limit)
        gaps[r] = gap + col_gap[...]
        limits[r] = limit

    prepare(0)
    pl.semaphore_wait(barrier, GRP + 3)
    for s in range(AHEAD):
        exchange(s)

    def step(t, _):
        @pl.when(t + AHEAD < NST)
        def _():
            exchange(t + AHEAD)

        @pl.when(t < NST)
        def _():
            multiply(t)

        @pl.when((t >= LAG_M) & (t < NST + LAG_M))
        def _():
            middle(t - LAG_M, 0)
            middle(t - LAG_M, 1)

        @pl.when((t >= LAG_S) & (t < NST + LAG_S))
        def _():
            second(t - LAG_S)

        @pl.when(t == NST)
        def _():
            for p in range(HELD):
                spread(p)

        @pl.when(t >= LAG_T)
        def _():
            third(t - LAG_T)

        @pl.when((t >= LAG_T + 2 * HELD) & (lax.rem(t - LAG_T, 2) == 1))
        def _():
            spread((t - LAG_T) // 2)

        @pl.when((t < NST - 1) & (lax.rem(t, 2) == 1))
        def _():
            prepare((t + 1) // 2)

        @pl.when(t < NST)
        def _():
            first(t)

        return 0

    lax.fori_loop(0, NST + LAG_T, step, 0)
    for p in range(NIRR):
        last(p)

    column = lax.broadcasted_iota(jnp.int32, (NIRR, COLS), 1)
    for r in range(R):
        out[r] = jnp.where(column < limits[r], -(cycle[r] + residual[r]) / gaps[r], 0.0)

    def drain(s, _):
        most = blocks.at[s, pl.ds(0, WIDE - CB)]
        pltpu.make_async_copy(most, most, x_ssem.at[s]).wait()
        core_copy(s).wait_send()
        for ph in range(2):
            for d in (0, 1):
                copy_1(s, ph, d).wait_send()
                both_2(s, ph, d).wait_send()
            for d in (1, 2, 3):
                copy_straight(s, ph, d).wait_send()
        return 0

    lax.fori_loop(0, NST, drain, 0)
    for p in range(NIRR):
        most = z_send.at[p, pl.ds(0, NZ - 1)]
        pltpu.make_async_copy(most, most, z_ssem.at[p]).wait()


def local(amps, integrals, residual_other, row_gap, col_gap, row_count, k_count, col_count):
    f32 = jnp.float32
    hbm = pl.BlockSpec(memory_space=pl.ANY)
    vmem, smem = pl.BlockSpec(memory_space=pltpu.VMEM), pl.BlockSpec(memory_space=pltpu.SMEM)
    return pl.pallas_call(
        kernel,
        out_shape=jax.ShapeDtypeStruct((R, NIRR, COLS), f32),
        in_specs=[hbm, hbm, hbm, hbm, smem, smem, smem, smem],
        out_specs=vmem,
        scratch_shapes=[
            pltpu.VMEM((R, NIRR, COLS), f32),
            pltpu.VMEM((NIRR, COLS), f32),
            pltpu.VMEM((NIRR, ROWS, KB), f32),
            pltpu.VMEM((NST, WIDE, KB), f32),
            pltpu.VMEM((ROWS, 2 * KB), jnp.bfloat16),
            pltpu.VMEM((2, WIDE, 2 * KB), jnp.bfloat16),
            pltpu.VMEM((NST, HALF, WIDE), f32),
            pltpu.VMEM((NST, HALF, WIDE), f32),
            pltpu.VMEM((HALF, WIDE), f32),
            pltpu.VMEM((NST, 4, 2, NX * PR // 2, LANES), f32),
            pltpu.VMEM((NST, 2, NX * PR // 2, LANES), f32),
            pltpu.VMEM((NST, 2, 2, NX * PR // 2, LANES), f32),
            pltpu.VMEM((NST, NX, PR, LANES), f32),
            pltpu.VMEM((NST, 3, PR, LANES), f32),
            pltpu.VMEM((NST, 4, 2, NY * QR // 2, LANES), f32),
            pltpu.VMEM((NST, 2, NY * QR // 2, LANES), f32),
            pltpu.VMEM((NST, 2, 2, NY * QR // 2, LANES), f32),
            pltpu.VMEM((NST, NY, QR, LANES), f32),
            pltpu.VMEM((NST, 3, QR, LANES), f32),
            pltpu.VMEM((NZ * R, WIDE), f32),
            pltpu.VMEM((NIRR, NZ, 2 * R, WIDE), f32),
            pltpu.VMEM((NIRR, NZ, 2 * R, WIDE), f32),
            pltpu.VMEM((R, NIRR, COLS), f32),
            pltpu.VMEM((R, NIRR, COLS), jnp.int32),
            pltpu.VMEM((R, NIRR, COLS), f32),
            pltpu.SemaphoreType.DMA((2,)),
            pltpu.SemaphoreType.DMA((NIRR,)),
            pltpu.SemaphoreType.DMA((NST,)),
            pltpu.SemaphoreType.DMA((NST,)),
            pltpu.SemaphoreType.DMA((NST,)),
            pltpu.SemaphoreType.DMA((NST,)),
            pltpu.SemaphoreType.DMA((NST, 8)),
            pltpu.SemaphoreType.DMA((NST, 8)),
            pltpu.SemaphoreType.DMA((NST, 6)),
            pltpu.SemaphoreType.DMA((NST, 6)),
            pltpu.SemaphoreType.DMA((NIRR,)),
            pltpu.SemaphoreType.DMA((NIRR,)),
        ],
        compiler_params=pltpu.CompilerParams(
            collective_id=0, has_side_effects=True, vmem_limit_bytes=56 * 2**20
        ),
        cost_estimate=pl.CostEstimate(
            flops=2 * NIRR * ROWS * COLS * KB * 4, bytes_accessed=6 * 2**20, transcendentals=0
        ),
    )(amps, jnp.swapaxes(integrals, 1, 2).reshape(NIRR, 2, CB, -1), residual_other, col_gap, row_gap, row_count, k_count, col_count)


def solution(mesh):
    return jax.shard_map(
        local,
        mesh=mesh,
        in_specs=(
            P(None, None, ("rep", "grp")),
            P(None, "rep", "grp"),
            P(("rep", "grp"), None, None),
            P(("rep", "grp"), None),
            P(),
            P(),
            P(),
            P(),
        ),
        out_specs=P(("rep", "grp"), None, None),
        check_vma=False,
    )
```

```python
import jax
import jax.numpy as jnp
from jax import lax
from jax.experimental import pallas as pl
from jax.experimental.pallas import tpu as pltpu
from jax.sharding import PartitionSpec as P

MESH = pl.DeviceIdType.MESH
NY, NC, NZ, NX = 4, 2, 8, 4
GRP = NZ * NX
NIRR = 8
ROWS = 1024
COLS = 512
KB = 128
R = 4
HALF = ROWS // NC
NST = 2 * NIRR
CB = 8
WIDE = GRP * CB
LANES = 128
UNITS = NZ * R * (WIDE // LANES)
PR = 48
QR = UNITS - PR
AHEAD = 6
LAG_M, LAG_S, LAG_T = 2, 4, 6
HELD = (NST - LAG_T) // 2


def kernel(
    amps, ints, residual_in, col_gap_in, row_gap, row_count, k_count, col_count, out,
    residual, col_gap, left, blocks, lhs, rhs, c_send, c_recv, c_mine,
    py_d, py_1, py_2, px_d, px_r,
    qx_d, qx_1, qx_2, qy_d, qy_r,
    f_even, z_send, z_recv, gaps, limits, cycle,
    i_sem, a_sem, x_ssem, x_rsem, c_ssem, c_rsem, p_ssem, p_rsem, d_ssem, d_rsem, z_ssem, z_rsem,
):
    rep, grp = lax.axis_index("rep"), lax.axis_index("grp")
    y, c = rep // NC, rep % NC
    z, x = grp // NX, grp % NX
    first_k = (rep * GRP + grp) * KB

    def swing(j, n):
        step = (j + 1) // 2
        return lax.rem(n // 2 + n + (1 - 2 * lax.rem(j, 2)) * step, n)

    def peer(d):
        return lax.rem(z + swing(d // NX, NZ), NZ) * NX + lax.rem(x + swing(lax.rem(d, NX), NX), NX)

    sibling = (y * NC + 1 - c, grp)

    def y_next(sign):
        return (lax.rem(y + sign, NY) * NC + c, grp)

    def x_next(sign):
        return (rep, z * NX + lax.rem(x + sign, NX))

    def z_peer(d):
        return lax.rem(z + d, NZ)

    def load(s):
        return pltpu.make_async_copy(amps.at[s], left.at[s], a_sem.at[s])

    for s in range(NIRR):
        load(s).start()
    inputs = (
        pltpu.make_async_copy(col_gap_in, col_gap, i_sem.at[0]),
        pltpu.make_async_copy(residual_in, residual, i_sem.at[1]),
    )
    for copy in inputs:
        copy.start()
    barrier = pltpu.get_barrier_semaphore()

    def greet(d, _):
        pl.semaphore_signal(barrier, inc=1, device_id=(rep, peer(d)), device_id_type=MESH)
        return 0

    lax.fori_loop(0, GRP - 1, greet, 0)
    for other in (sibling, y_next(1), y_next(2), y_next(3)):
        pl.semaphore_signal(barrier, inc=1, device_id=other, device_id_type=MESH)

    def own_block(s):
        return pltpu.make_async_copy(
            ints.at[s // 2, lax.rem(s, 2), :, pl.ds(pl.multiple_of(grp * KB, KB), KB)],
            blocks.at[s, pl.ds(pl.multiple_of(grp * CB, CB), CB)],
            x_rsem.at[s],
        )

    def exchange(s):
        own_block(s).start()

        def send(d, _):
            to = peer(d)
            pltpu.make_async_remote_copy(
                ints.at[s // 2, lax.rem(s, 2), :, pl.ds(pl.multiple_of(to * KB, KB), KB)],
                blocks.at[s, pl.ds(pl.multiple_of(grp * CB, CB), CB)],
                x_ssem.at[s],
                x_rsem.at[s],
                device_id=(rep, to),
                device_id_type=MESH,
            ).start()
            return 0

        lax.fori_loop(0, GRP - 1, send, 0)

    def copy_1(s, ph, d):
        data, one, _, me, nxt = phases[ph]
        return pltpu.make_async_remote_copy(
            data.at[s, lax.rem(me + 2, 4), d],
            one.at[s, d],
            p_ssem.at[s, ph * 4 + d],
            p_rsem.at[s, ph * 4 + d],
            device_id=nxt(1 + 2 * d),
            device_id_type=MESH,
        )

    def copy_2(s, ph, d, h):
        data, _, two, me, nxt = phases[ph]
        return pltpu.make_async_remote_copy(
            data.at[s, lax.rem(me + (1, 3)[d], 4), h],
            two.at[s, d, h],
            p_ssem.at[s, ph * 4 + 2 + d],
            p_rsem.at[s, ph * 4 + 2 + d],
            device_id=nxt(1 + 2 * d),
            device_id_type=MESH,
        )

    def both_2(s, ph, d):
        _, _, two, _, nxt = phases[ph]
        return pltpu.make_async_remote_copy(
            two.at[s, d],
            two.at[s, d],
            p_ssem.at[s, ph * 4 + 2 + d],
            p_rsem.at[s, ph * 4 + 2 + d],
            device_id=nxt(1 + 2 * d),
            device_id_type=MESH,
        )

    phases = (
        (py_d, py_1, py_2, y, y_next),
        (qx_d, qx_1, qx_2, x, x_next),
    )

    def begin(s, ph):
        for d in (0, 1):
            copy_1(s, ph, d).start()
        for d in (0, 1):
            copy_2(s, ph, d, 1 - d).start()

    def middle(s, ph):
        data, one, _, me, _ = phases[ph]
        for d in (0, 1):
            copy_1(s, ph, d).wait_recv()
            at = lax.rem(me + (1, 3)[d], 4)
            data[s, at, d] = data[s, at, d] + one[s, d]
            copy_2(s, ph, d, d).start()

    def end(s, ph):
        data, _, two, me, _ = phases[ph]
        for d in (0, 1):
            both_2(s, ph, d).wait_recv()
        return data[s, me] + two[s, 0] + two[s, 1]

    straight = ((px_d, px_r, x, x_next), (qy_d, qy_r, y, y_next))

    def copy_straight(s, ph, d):
        data, got, me, nxt = straight[ph]
        return pltpu.make_async_remote_copy(
            data.at[s, lax.rem(me + d, 4)],
            got.at[s, d - 1],
            d_ssem.at[s, ph * 3 + d - 1],
            d_rsem.at[s, ph * 3 + d - 1],
            device_id=nxt(d),
            device_id_type=MESH,
        )

    def begin_straight(s, ph):
        for d in (2, 1, 3):
            copy_straight(s, ph, d).start()

    def end_straight(s, ph):
        data, got, me, _ = straight[ph]
        for d in (1, 2, 3):
            copy_straight(s, ph, d).wait_recv()
        return data[s, me] + got[s, 0] + got[s, 1] + got[s, 2]

    def core_copy(s, i):
        return pltpu.make_async_remote_copy(
            c_send.at[s, i], c_recv.at[s, i], c_ssem.at[s, i], c_rsem.at[s, i], device_id=sibling, device_id_type=MESH
        )

    def prepare(s):
        load(s).wait()
        low = (lax.broadcasted_iota(jnp.int32, (128, KB), 0) % 8) < 4

        def block(i, _):
            yy, cc = i // NC, lax.rem(i, NC)
            a = left[s, pl.ds(pl.multiple_of(i * 128, 128), 128)]
            shape = (NZ // 2, 2, NX // 2, 8, KB)
            down = pltpu.roll(a, 4, 0)
            up = pltpu.roll(a, 124, 0)
            a5, d5, u5, l5 = (v.reshape(shape) for v in (a, down, up, low))
            even = jnp.where(l5[:, 0], a5[:, 0], d5[:, 1])
            odd = jnp.where(l5[:, 0], u5[:, 0], a5[:, 1])
            rows = jnp.concatenate(
                [v[:, p].reshape(NZ * R, KB) for p in range(NX // 2) for v in (even, odd)], axis=0
            )
            hi = rows.astype(jnp.bfloat16)
            lo = (rows - hi.astype(jnp.float32)).astype(jnp.bfloat16)
            lhs[pl.ds(pl.multiple_of(cc * HALF + yy * 128, 128), 128)] = jnp.concatenate([hi, lo], axis=1)
            return 0

        lax.fori_loop(0, NY * NC, block, 0)

    def product(half, i):
        part = HALF // 2
        rows = lhs[pl.ds(pl.multiple_of(half * HALF + i * part, part), part)]
        dims = (((1,), (1,)), ((), ()))
        return lax.dot_general(rows, rhs[0], dims, preferred_element_type=jnp.float32) + lax.dot_general(
            rows, rhs[1], dims, preferred_element_type=jnp.float32
        )

    def multiply(s):
        pltpu.make_async_copy(blocks.at[s], blocks.at[s], x_rsem.at[s]).wait()
        k_index = first_k + lax.broadcasted_iota(jnp.int32, (WIDE, KB), 1)
        b = jnp.where(k_index < k_count[s // 2], blocks[s], 0.0)
        hi = b.astype(jnp.bfloat16)
        lo = (b - hi.astype(jnp.float32)).astype(jnp.bfloat16)
        rhs[0] = jnp.concatenate([hi, hi], axis=1)
        rhs[1] = jnp.concatenate([lo, lo], axis=1)
        for i in (0, 1):
            c_send[s, i] = product(1 - c, i)
            core_copy(s, i).start()
        for i in (0, 1):
            c_mine[i] = product(c, i)

    def first(s):
        for i in (0, 1):
            core_copy(s, i).wait_recv()
        total = (c_mine[...] + c_recv[s]).reshape(NY, NX, NZ * R, WIDE)
        total = jnp.concatenate([total[..., :LANES], total[..., LANES:]], axis=2)
        py_d[s] = total[:, :, :PR].reshape(NY, 2, NX * PR // 2, LANES)
        begin(s, 0)
        for xx in range(NX):
            qx_d[s, xx] = total[:, xx, PR:].reshape(2, NY * QR // 2, LANES)
        begin(s, 1)

    def second(s):
        px_d[s] = end(s, 0).reshape(NX, PR, LANES)
        begin_straight(s, 0)
        qy_d[s] = end(s, 1).reshape(NY, QR, LANES)
        begin_straight(s, 1)

    def z_copy(p, d):
        to = z_peer(d)
        return pltpu.make_async_remote_copy(
            z_send.at[p, to],
            z_recv.at[p, z],
            z_ssem.at[p],
            z_rsem.at[p],
            device_id=(rep, to * NX + x),
            device_id_type=MESH,
        )

    def third(s):
        f = jnp.concatenate([end_straight(s, 0), end_straight(s, 1)], axis=0)
        f = jnp.concatenate([f[: NZ * R], f[NZ * R :]], axis=1)

        @pl.when(lax.rem(s, 2) == 0)
        def _():
            f_even[...] = f

        @pl.when(lax.rem(s, 2) == 1)
        def _():
            p = s // 2
            e = f_even[...]
            low = (lax.broadcasted_iota(jnp.int32, f.shape, 0) % 8) < 4
            z_even = jnp.where(low, e, pltpu.roll(f, 4, 0)).reshape(NZ // 2, 8, WIDE)
            z_odd = jnp.where(low, pltpu.roll(e, NZ * R - 4, 0), f).reshape(NZ // 2, 8, WIDE)
            for i in range(NZ // 2):
                z_send[p, 2 * i] = z_even[i]
                z_send[p, 2 * i + 1] = z_odd[i]

    def spread(p):
        pltpu.make_async_copy(z_send.at[p, z], z_recv.at[p, z], z_rsem.at[p]).start()
        for d in (4, 3, 5, 2, 6, 1, 7):
            z_copy(p, d).start()

    lane = lax.broadcasted_iota(jnp.int32, (2 * R, LANES), 1)

    def last(p):
        pltpu.make_async_copy(z_recv.at[p], z_recv.at[p], z_rsem.at[p]).wait()
        total = z_recv[p, 0]
        for i in range(1, NZ):
            total = total + z_recv[p, i]
        for q in range(COLS // LANES):
            part = total[:, LANES * (q // 2) : LANES * (q // 2 + 1)]
            both = jnp.zeros((2 * R, LANES), jnp.float32)
            for k in range(9):
                moved = pltpu.roll(part, (CB * k - 64 * (q % 2)) % LANES, 1)
                both = jnp.where((lane >= 16 * k - CB) & (lane < 16 * k + CB), moved, both)
            rows = jnp.where(lane % 16 < CB, both, pltpu.roll(both, R, 0))
            for r in range(R):
                cycle[r, p : p + 1, LANES * q : LANES * (q + 1)] = rows[r : r + 1]

    for copy in inputs:
        copy.wait()
    first_row = (rep * GRP + grp) * R
    irrep = lax.broadcasted_iota(jnp.int32, (NIRR, COLS), 0)
    for r in range(R):
        gap = jnp.zeros((NIRR, COLS), jnp.float32)
        limit = jnp.zeros((NIRR, COLS), jnp.int32)
        for s in range(NIRR):
            gap = jnp.where(irrep == s, row_gap[r, s], gap)
            limit = jnp.where(irrep == s, jnp.where(first_row + r < row_count[s], col_count[s], 0), limit)
        gaps[r] = gap + col_gap[...]
        limits[r] = limit

    prepare(0)
    pl.semaphore_wait(barrier, GRP + 3)
    for s in range(AHEAD):
        exchange(s)

    def step(t, _):
        @pl.when(t + AHEAD < NST)
        def _():
            exchange(t + AHEAD)

        @pl.when(t < NST)
        def _():
            multiply(t)

        @pl.when((t >= LAG_M) & (t < NST + LAG_M))
        def _():
            middle(t - LAG_M, 0)
            middle(t - LAG_M, 1)

        @pl.when((t >= LAG_S) & (t < NST + LAG_S))
        def _():
            second(t - LAG_S)

        @pl.when(t == NST)
        def _():
            for p in range(HELD):
                spread(p)

        @pl.when(t >= LAG_T)
        def _():
            third(t - LAG_T)

        @pl.when((t >= LAG_T + 2 * HELD) & (lax.rem(t - LAG_T, 2) == 1))
        def _():
            spread((t - LAG_T) // 2)

        @pl.when((t < NST - 1) & (lax.rem(t, 2) == 1))
        def _():
            prepare((t + 1) // 2)

        @pl.when(t < NST)
        def _():
            first(t)

        return 0

    lax.fori_loop(0, NST + LAG_T, step, 0)
    for p in range(NIRR):
        last(p)

    column = lax.broadcasted_iota(jnp.int32, (NIRR, COLS), 1)
    for r in range(R):
        out[r] = jnp.where(column < limits[r], -(cycle[r] + residual[r]) / gaps[r], 0.0)

    def drain(s, _):
        most = blocks.at[s, pl.ds(0, WIDE - CB)]
        pltpu.make_async_copy(most, most, x_ssem.at[s]).wait()
        for i in (0, 1):
            core_copy(s, i).wait_send()
        for ph in range(2):
            for d in (0, 1):
                copy_1(s, ph, d).wait_send()
                both_2(s, ph, d).wait_send()
            for d in (1, 2, 3):
                copy_straight(s, ph, d).wait_send()
        return 0

    lax.fori_loop(0, NST, drain, 0)
    for p in range(NIRR):
        most = z_send.at[p, pl.ds(0, NZ - 1)]
        pltpu.make_async_copy(most, most, z_ssem.at[p]).wait()


def local(amps, integrals, residual_other, row_gap, col_gap, row_count, k_count, col_count):
    f32 = jnp.float32
    hbm = pl.BlockSpec(memory_space=pl.ANY)
    vmem, smem = pl.BlockSpec(memory_space=pltpu.VMEM), pl.BlockSpec(memory_space=pltpu.SMEM)
    return pl.pallas_call(
        kernel,
        out_shape=jax.ShapeDtypeStruct((R, NIRR, COLS), f32),
        in_specs=[hbm, hbm, hbm, hbm, smem, smem, smem, smem],
        out_specs=vmem,
        scratch_shapes=[
            pltpu.VMEM((R, NIRR, COLS), f32),
            pltpu.VMEM((NIRR, COLS), f32),
            pltpu.VMEM((NIRR, ROWS, KB), f32),
            pltpu.VMEM((NST, WIDE, KB), f32),
            pltpu.VMEM((ROWS, 2 * KB), jnp.bfloat16),
            pltpu.VMEM((2, WIDE, 2 * KB), jnp.bfloat16),
            pltpu.VMEM((NST, 2, HALF // 2, WIDE), f32),
            pltpu.VMEM((NST, 2, HALF // 2, WIDE), f32),
            pltpu.VMEM((2, HALF // 2, WIDE), f32),
            pltpu.VMEM((NST, 4, 2, NX * PR // 2, LANES), f32),
            pltpu.VMEM((NST, 2, NX * PR // 2, LANES), f32),
            pltpu.VMEM((NST, 2, 2, NX * PR // 2, LANES), f32),
            pltpu.VMEM((NST, NX, PR, LANES), f32),
            pltpu.VMEM((NST, 3, PR, LANES), f32),
            pltpu.VMEM((NST, 4, 2, NY * QR // 2, LANES), f32),
            pltpu.VMEM((NST, 2, NY * QR // 2, LANES), f32),
            pltpu.VMEM((NST, 2, 2, NY * QR // 2, LANES), f32),
            pltpu.VMEM((NST, NY, QR, LANES), f32),
            pltpu.VMEM((NST, 3, QR, LANES), f32),
            pltpu.VMEM((NZ * R, WIDE), f32),
            pltpu.VMEM((NIRR, NZ, 2 * R, WIDE), f32),
            pltpu.VMEM((NIRR, NZ, 2 * R, WIDE), f32),
            pltpu.VMEM((R, NIRR, COLS), f32),
            pltpu.VMEM((R, NIRR, COLS), jnp.int32),
            pltpu.VMEM((R, NIRR, COLS), f32),
            pltpu.SemaphoreType.DMA((2,)),
            pltpu.SemaphoreType.DMA((NIRR,)),
            pltpu.SemaphoreType.DMA((NST,)),
            pltpu.SemaphoreType.DMA((NST,)),
            pltpu.SemaphoreType.DMA((NST, 2)),
            pltpu.SemaphoreType.DMA((NST, 2)),
            pltpu.SemaphoreType.DMA((NST, 8)),
            pltpu.SemaphoreType.DMA((NST, 8)),
            pltpu.SemaphoreType.DMA((NST, 6)),
            pltpu.SemaphoreType.DMA((NST, 6)),
            pltpu.SemaphoreType.DMA((NIRR,)),
            pltpu.SemaphoreType.DMA((NIRR,)),
        ],
        compiler_params=pltpu.CompilerParams(
            collective_id=0, has_side_effects=True, vmem_limit_bytes=56 * 2**20
        ),
        cost_estimate=pl.CostEstimate(
            flops=2 * NIRR * ROWS * COLS * KB * 4, bytes_accessed=6 * 2**20, transcendentals=0
        ),
    )(amps, jnp.swapaxes(integrals, 1, 2).reshape(NIRR, 2, CB, -1), residual_other, col_gap, row_gap, row_count, k_count, col_count)


def solution(mesh):
    return jax.shard_map(
        local,
        mesh=mesh,
        in_specs=(
            P(None, None, ("rep", "grp")),
            P(None, "rep", "grp"),
            P(("rep", "grp"), None, None),
            P(("rep", "grp"), None),
            P(),
            P(),
            P(),
            P(),
        ),
        out_specs=P(("rep", "grp"), None, None),
        check_vma=False,
    )
```
